1024 devices in a mesh: dp: 16 (over y, core), fsdp: 16 (over z), mp: 4 (over x).
Axes of the slice: x: 4, y: 8, z: 16, core: 2. Of those that a mesh axis runs over, the one named last changes fastest.
Arguments:
- gradient: bfloat16 [16, 4, 16, 512, 256], P('dp', 'mp', None, 'fsdp'), may hold values from -6 to 6
- owner_table: int32 [8, 4, 16], P(None, 'mp'), may hold values from 0 to 15, each once within a row
- refresh: int32 [16, 4, 16], P('dp', 'mp', 'fsdp'), may hold values from 0 to 1, as said below
- statistics: float32 [16, 4, 16, 512, 512], P('dp', 'mp', 'fsdp'), may hold values from -1 to 5, as said below
- inv_roots: bfloat16 [16, 4, 16, 512, 512], P('dp', 'mp', 'fsdp'), may hold values from -1 to 3, as said below
Outputs:
- update: bfloat16 [16, 4, 16, 512, 256], P('dp', 'mp', None, 'fsdp')
- new_stats: float32 [16, 4, 16, 512, 512], P('dp', 'mp', 'fsdp')
The draws below stay inside these ranges and needn't reach their ends.
Inputs may be any that keep to these rules, and one draw needn't show every extreme that they name: `owner_table`: for each block column, a permutation of the 16 block rows onto the owner slots. `refresh`: for each side, block column group and slot, exactly one of the 4 mp indices is 1. `statistics`: every matrix is symmetric with a positive diagonal. `inv_roots`: every matrix is symmetric with a positive diagonal.
All inputs are finite; a program needn't handle non-finite values. Where the reference program divides by a largest or mean magnitude, that divisor is 1e-20 or more.
Results may differ from the reference program's by a relative error of at most 0.0059.
Values may be sent and summed in bfloat16 or wider, within the bound.
No kernel may reach another device: no remote copies, remote signals or barrier semaphores. Data moves between devices by JAX's collectives and lax.ppermute only.
A program may use at most 32 MiB of HBM per device.

```python
import math
import jax
import jax.numpy as jnp
from jax import lax

B = 512
ITERS = 2
NBR = 16
KPM = 8
N_MP = 4


def symmetric_blocks(key, low_diag, high_diag, amplitude):
    scale_key, noise_key = jax.random.split(key)
    diag_vals = jnp.exp(jax.random.uniform(scale_key, (2 * KPM, N_MP, NBR, B), jnp.float32, math.log(low_diag), math.log(high_diag)))
    noise = jax.random.uniform(noise_key, (2 * KPM, N_MP, NBR, B, B), jnp.float32, -1.0, 1.0)
    sym_noise = (noise + jnp.swapaxes(noise, -1, -2)) * (0.5 * amplitude)
    root_diag = jnp.sqrt(diag_vals)
    identity = jnp.eye(B, dtype=jnp.float32)
    return root_diag[..., :, None] * (identity + sym_noise) * root_diag[..., None, :]


def draw_refresh(key, part):
    key = jax.random.fold_in(key, 37)
    picked = jax.random.randint(key, (2 * KPM, NBR), 0, N_MP)
    return (jnp.arange(N_MP)[None, :, None] == picked[:, None, :]).astype(jnp.int32)


def draw_statistics(key, part):
    key = jax.random.fold_in(key, 11)
    return symmetric_blocks(key, 0.3, 3.0, 0.8 / math.sqrt(B))


def draw_inv_roots(key, part):
    key = jax.random.fold_in(key, 23)
    return symmetric_blocks(key, 0.5, 2.0, 0.5 / math.sqrt(B)).astype(jnp.bfloat16)


def block_levels(key, extent, pieces, least, top_value):
    def one(position, shards_of):
        draws = jax.random.uniform(jax.random.fold_in(jax.random.fold_in(key, 6), position), (shards_of,), jnp.float32, least / len(pieces), top_value / len(pieces))
        return jnp.repeat(jnp.exp(draws), extent[position] // shards_of).reshape((-1,) + (1,) * (len(extent) - position - 1))

    factor_of = one(*pieces[0])
    for cut in pieces[1:]:
        factor_of = factor_of * one(*cut)
    return factor_of


def gaussian(key, shape, spread, bound, shards=(), kind=jnp.bfloat16):
    values = spread * jax.random.normal(key, shape, jnp.float32)
    if shards:
        values = values * block_levels(key, shape, shards, -0.22, 0.18)
    return jnp.clip(values, -bound, bound).astype(kind)


def setup_inputs(seed: int = 0) -> dict:
    key_list = jax.random.split(jax.random.key(seed), 6)
    return {
        "gradient": gaussian(key_list[0], (2 * KPM, N_MP, NBR, B, B // 2), 1.0, 6.0, ((0, 16), (1, 4), (3, 16))),
        "owner_table": jax.vmap(lambda own: jax.random.permutation(own, NBR))(jax.random.split(key_list[1], KPM * N_MP)).reshape((KPM, N_MP, NBR)).astype(jnp.int32),
        "refresh": draw_refresh(jax.random.fold_in(key_list[5], 71), 0),
        "statistics": draw_statistics(jax.random.fold_in(key_list[5], 71), 0),
        "inv_roots": draw_inv_roots(jax.random.fold_in(key_list[5], 71), 0),
    }


stat_decay = 0.9


def newton_root(matrix):
    identity = jnp.eye(matrix.shape[-1], dtype=jnp.float32)
    row_bound = jnp.max(jnp.sum(jnp.abs(matrix), axis=1))
    scaling = 2.5 / row_bound
    iterate = scaling * matrix
    root_est = jnp.zeros_like(matrix)
    for newton_turn in range(ITERS):
        step_mat = ((5.0 * identity - iterate) * 0.25).astype(jnp.bfloat16)
        if newton_turn == 0:
            root_est = scaling ** 0.25 * lax.optimization_barrier(step_mat).astype(jnp.float32)
        else:
            root_est = jnp.dot(root_est.astype(jnp.bfloat16), step_mat, preferred_element_type=jnp.float32)
        if newton_turn + 1 < ITERS:
            square = jnp.dot(step_mat, step_mat, preferred_element_type=jnp.float32).astype(jnp.bfloat16)
            fourth = jnp.dot(square, square, preferred_element_type=jnp.float32).astype(jnp.bfloat16)
            iterate = jnp.dot(fourth, iterate.astype(jnp.bfloat16), preferred_element_type=jnp.float32)
    return root_est.astype(jnp.bfloat16)


def one_slot(slot_items):
    block_grad, left_stat, right_stat, left_old, right_old, left_flag, right_flag = slot_items
    left_new = stat_decay * left_stat + (1.0 - stat_decay) / B * jnp.dot(block_grad, block_grad.T, preferred_element_type=jnp.float32)
    right_new = stat_decay * right_stat + (1.0 - stat_decay) / B * jnp.dot(block_grad.T, block_grad, preferred_element_type=jnp.float32)
    left_root = jnp.where(left_flag == 1, newton_root(left_stat), left_old)
    right_root = jnp.where(right_flag == 1, newton_root(right_stat), right_old)
    partial_value = jnp.dot(left_root, block_grad, preferred_element_type=jnp.float32).astype(jnp.bfloat16)
    result = jnp.dot(partial_value, right_root, preferred_element_type=jnp.float32).astype(jnp.bfloat16)
    return left_new, right_new, result


def reference(gradient, owner_table, refresh, statistics, inv_roots):
    blocks = gradient.reshape(2, KPM, N_MP, NBR, B, B // 2)
    blocks = blocks.transpose(1, 2, 3, 4, 0, 5).reshape(KPM, N_MP, NBR, B, B)
    inverse = jnp.argsort(owner_table, axis=2).astype(jnp.int32)
    by_slot = jnp.take_along_axis(blocks, inverse[:, :, :, None, None], axis=2)
    slot_count = KPM * N_MP * NBR
    flat_blocks = by_slot.reshape(slot_count, B, B)
    stat_pairs = statistics.reshape(2, slot_count, B, B)
    root_pairs = inv_roots.reshape(2, slot_count, B, B)
    flag_pairs = refresh.reshape(2, slot_count)
    left_new, right_new, result = lax.map(
        one_slot, (flat_blocks, stat_pairs[0], stat_pairs[1], root_pairs[0], root_pairs[1], flag_pairs[0], flag_pairs[1]))
    new_stats = jnp.concatenate([left_new, right_new], axis=0).reshape(2 * KPM, N_MP, NBR, B, B)
    result = result.reshape(KPM, N_MP, NBR, B, B)
    in_blocks = jnp.take_along_axis(result, owner_table.astype(jnp.int32)[:, :, :, None, None], axis=2)
    update = in_blocks.reshape(KPM, N_MP, NBR, B, 2, B // 2).transpose(4, 0, 1, 2, 3, 5)
    update = update.reshape(2 * KPM, N_MP, NBR, B, B // 2)
    return update, new_stats
```

```python
import functools

import jax
import jax.numpy as jnp
from jax import lax
from jax.experimental import pallas as pl
from jax.experimental.pallas import tpu as pltpu
from jax.sharding import PartitionSpec as P

ITERS = 2
STAT_DECAY = 0.9
MIB = 1024 * 1024

VMEM = pl.BlockSpec(memory_space=pltpu.VMEM)
SMEM = pl.BlockSpec(memory_space=pltpu.SMEM)
ANY = pl.BlockSpec(memory_space=pl.ANY)


def dot(left, right, contract=((1,), (0,))):
    return lax.dot_general(left, right, (contract, ((), ())), preferred_element_type=jnp.float32)


def flip(block):
    return block.astype(jnp.float32).T.astype(block.dtype)


def to_slots_kernel(groups, table_ref, grad_ref, out_ref, sems):
    group = lax.rem(lax.axis_index("dp"), groups)
    copies = []
    for r in range(grad_ref.shape[0]):
        slot = table_ref[group, 0, r]
        copies.append(pltpu.make_async_copy(grad_ref.at[r], out_ref.at[slot], sems.at[r]))
        copies[-1].start()
    for copy in copies:
        copy.wait()


def from_slots_kernel(groups, table_ref, got_ref, out_ref, sems):
    group = lax.rem(lax.axis_index("dp"), groups)
    copies = []
    for r in range(out_ref.shape[0]):
        slot = table_ref[group, 0, r]
        copies.append(pltpu.make_async_copy(got_ref.at[slot], out_ref.at[r], sems.at[r]))
        copies[-1].start()
    for copy in copies:
        copy.wait()


def move_blocks(body, groups, table, blocks):
    return pl.pallas_call(
        functools.partial(body, groups),
        out_shape=jax.ShapeDtypeStruct(blocks.shape, blocks.dtype),
        in_specs=[SMEM, ANY],
        out_specs=ANY,
        scratch_shapes=[pltpu.SemaphoreType.DMA((blocks.shape[0],))],
        compiler_params=pltpu.CompilerParams(vmem_limit_bytes=MIB),
        cost_estimate=pl.CostEstimate(flops=0, bytes_accessed=2 * blocks.size * 2, transcendentals=0),
    )(table, blocks)


def root_kernel(flag_ref, stat_ref, old_ref, root_ref, pack_ref):
    order = stat_ref.shape[0]
    half = order // 2

    @pl.when(flag_ref[0, 0, 0] == 1)
    def _():
        matrix = stat_ref[...]
        rows = lax.broadcasted_iota(jnp.int32, (order, order), 0)
        cols = lax.broadcasted_iota(jnp.int32, (order, order), 1)
        on_diag = rows == cols
        bound = jnp.max(jnp.sum(jnp.abs(matrix), axis=0, keepdims=True), axis=1, keepdims=True)
        scaling = 2.5 / bound
        iterate = scaling * matrix
        root = None
        for turn in range(ITERS):
            step = (jnp.where(on_diag, 5.0 - iterate, -iterate) * 0.25).astype(jnp.bfloat16)
            if turn == 0:
                root = jnp.sqrt(jnp.sqrt(scaling)) * step.astype(jnp.float32)
            else:
                root = dot(root.astype(jnp.bfloat16), step)
            if turn + 1 < ITERS:
                square = dot(step, step).astype(jnp.bfloat16)
                fourth = dot(square, square).astype(jnp.bfloat16)
                iterate = dot(fourth, iterate.astype(jnp.bfloat16))
        root_ref[...] = root.astype(jnp.bfloat16)

    @pl.when(flag_ref[0, 0, 0] != 1)
    def _():
        root_ref[...] = old_ref[...]

    rows = lax.broadcasted_iota(jnp.int32, (half, half), 0)
    cols = lax.broadcasted_iota(jnp.int32, (half, half), 1)
    first = root_ref[0:half, 0:half].astype(jnp.float32)
    second = root_ref[half:order, half:order].astype(jnp.float32)
    pack_ref[0:half, :] = jnp.where(rows <= cols, first, second).astype(jnp.bfloat16)
    pack_ref[half:order, :] = root_ref[half:order, 0:half]
    diagonal = jnp.sum(jnp.where(rows == cols, second, 0.0), axis=0, keepdims=True)
    pack_ref[order : order + 16, :] = jnp.broadcast_to(diagonal, (16, half)).astype(jnp.bfloat16)


def fresh_and_packed(flag, stat, old):
    order = stat.shape[0]
    return pl.pallas_call(
        root_kernel,
        out_shape=(
            jax.ShapeDtypeStruct((order, order), jnp.bfloat16),
            jax.ShapeDtypeStruct((order + 16, order // 2), jnp.bfloat16),
        ),
        in_specs=[SMEM, VMEM, VMEM],
        out_specs=(VMEM, VMEM),
        compiler_params=pltpu.CompilerParams(vmem_limit_bytes=24 * MIB),
        cost_estimate=pl.CostEstimate(flops=8 * order**3, bytes_accessed=9 * order**2, transcendentals=0),
    )(flag, stat, old)


def own_kernel(half_group, root_ref, pack_ref, own_ref, left_ref, right_ref, partial_ref):
    order = root_ref.shape[0]
    half = order // 2
    side = lax.axis_index("dp") // half_group
    rows = lax.broadcasted_iota(jnp.int32, (half, half), 0)
    cols = lax.broadcasted_iota(jnp.int32, (half, half), 1)
    tri = pack_ref[0:half, :].astype(jnp.float32)
    tri_flipped = tri.T
    first = jnp.where(rows <= cols, tri, tri_flipped).astype(jnp.bfloat16)

    @pl.when(side == 0)
    def _():
        left_ref[...] = root_ref[...]
        right_ref[0:half, :] = first
        right_ref[half:order, :] = pack_ref[half:order, :]

    @pl.when(side != 0)
    def _():
        right_ref[...] = root_ref[:, half:order]
        diagonal = pack_ref[order : order + 16, :].astype(jnp.float32)[0:1, :]
        second = jnp.where(rows > cols, tri, jnp.where(rows == cols, diagonal, tri_flipped))
        left_ref[0:half, 0:half] = first
        left_ref[half:order, half:order] = second.astype(jnp.bfloat16)
        left_ref[half:order, 0:half] = pack_ref[half:order, :]
        left_ref[0:half, half:order] = flip(pack_ref[half:order, :])

    partial_ref[...] = dot(left_ref[...], own_ref[...]).astype(jnp.bfloat16)


def own_part(half_group, root, pack, own):
    order = root.shape[0]
    half = order // 2
    return pl.pallas_call(
        functools.partial(own_kernel, half_group),
        out_shape=(
            jax.ShapeDtypeStruct((order, order), jnp.bfloat16),
            jax.ShapeDtypeStruct((order, half), jnp.bfloat16),
            jax.ShapeDtypeStruct((order, half), jnp.bfloat16),
        ),
        in_specs=[VMEM] * 3,
        out_specs=(VMEM,) * 3,
        compiler_params=pltpu.CompilerParams(vmem_limit_bytes=16 * MIB),
        cost_estimate=pl.CostEstimate(flops=order**3, bytes_accessed=6 * order**2, transcendentals=0),
    )(root, pack, own)


def result_kernel(half_group, left_ref, right_ref, partial_ref, other_ref, out_ref):
    order = left_ref.shape[0]
    half = order // 2
    side = lax.axis_index("dp") // half_group
    mine = pl.ds(pl.multiple_of(side * half, half), half)
    theirs = pl.ds(pl.multiple_of((1 - side) * half, half), half)
    other_partial = dot(left_ref[...], other_ref[...]).astype(jnp.bfloat16)
    total = dot(partial_ref[...], right_ref[mine, :]) + dot(other_partial, right_ref[theirs, :])
    out_ref[...] = total.astype(jnp.bfloat16)


def result_half(half_group, left, right, partial, other):
    order = left.shape[0]
    return pl.pallas_call(
        functools.partial(result_kernel, half_group),
        out_shape=jax.ShapeDtypeStruct(other.shape, jnp.bfloat16),
        in_specs=[VMEM] * 4,
        out_specs=VMEM,
        compiler_params=pltpu.CompilerParams(vmem_limit_bytes=16 * MIB),
        cost_estimate=pl.CostEstimate(flops=2 * order**3, bytes_accessed=6 * order**2, transcendentals=0),
    )(left, right, partial, other)


def stats_kernel(half_group, stat_ref, own_ref, other_ref, out_ref):
    order = stat_ref.shape[0]
    half = order // 2
    side = lax.axis_index("dp") // half_group
    factor = (1.0 - STAT_DECAY) / order

    @pl.when(side == 0)
    def _():
        own, other = own_ref[...], other_ref[...]
        gram = dot(own, own, ((1,), (1,))) + dot(other, other, ((1,), (1,)))
        out_ref[...] = STAT_DECAY * stat_ref[...] + factor * gram

    @pl.when(side != 0)
    def _():
        halves = (other_ref[...], own_ref[...])
        for i in range(2):
            lines = slice(i * half, (i + 1) * half)
            turned = flip(halves[i])
            for j in range(2):
                columns = slice(j * half, (j + 1) * half)
                gram = dot(turned, halves[j])
                out_ref[lines, columns] = STAT_DECAY * stat_ref[lines, columns] + factor * gram


def updated_stats(half_group, stat, own, other):
    order = stat.shape[0]
    return pl.pallas_call(
        functools.partial(stats_kernel, half_group),
        out_shape=jax.ShapeDtypeStruct(stat.shape, jnp.float32),
        in_specs=[VMEM] * 3,
        out_specs=VMEM,
        compiler_params=pltpu.CompilerParams(vmem_limit_bytes=16 * MIB),
        cost_estimate=pl.CostEstimate(flops=2 * order**3, bytes_accessed=10 * order**2, transcendentals=0),
    )(stat, own, other)


def shards(gradient, owner_table, refresh, statistics, inv_roots):
    order = statistics.shape[-1]
    half = order // 2
    dp_count = lax.axis_size("dp")
    half_group = dp_count // 2
    swap = [(source, (source + half_group) % dp_count) for source in range(dp_count)]
    stat = statistics[0, 0, 0]
    outgoing = move_blocks(to_slots_kernel, half_group, owner_table, gradient[0, 0])
    received = lax.all_to_all(outgoing, "fsdp", split_axis=0, concat_axis=0, tiled=True)
    own = received.reshape(order, half)
    root, pack = fresh_and_packed(refresh, stat, inv_roots[0, 0, 0])
    other_pack = lax.ppermute(pack, "dp", swap)
    own, pack = lax.optimization_barrier((own, pack))
    other = lax.ppermute(own, "dp", swap)
    left, right, partial = own_part(half_group, root, other_pack, own)
    result = result_half(half_group, left, right, partial, other)
    result, own, other = lax.optimization_barrier((result, own, other))
    returned = lax.all_to_all(result.reshape(outgoing.shape), "fsdp", split_axis=0, concat_axis=0, tiled=True)
    new_stat = updated_stats(half_group, stat, own, other)
    update = move_blocks(from_slots_kernel, half_group, owner_table, returned)
    return update[None, None], new_stat[None, None, None]


def solution(mesh):
    return jax.shard_map(
        shards,
        mesh=mesh,
        in_specs=(
            P("dp", "mp", None, "fsdp", None),
            P(None, "mp", None),
            P("dp", "mp", "fsdp"),
            P("dp", "mp", "fsdp", None, None),
            P("dp", "mp", "fsdp", None, None),
        ),
        out_specs=(P("dp", "mp", None, "fsdp", None), P("dp", "mp", "fsdp", None, None)),
        check_vma=False,
    )
```

```python
import functools

import jax
import jax.numpy as jnp
from jax import lax
from jax.experimental import pallas as pl
from jax.experimental.pallas import tpu as pltpu
from jax.sharding import PartitionSpec as P

ITERS = 2
STAT_DECAY = 0.9
MIB = 1024 * 1024

VMEM = pl.BlockSpec(memory_space=pltpu.VMEM)
SMEM = pl.BlockSpec(memory_space=pltpu.SMEM)
HBM = pl.BlockSpec(memory_space=pltpu.HBM)


def dot(left, right, contract=((1,), (0,))):
    return lax.dot_general(left, right, (contract, ((), ())), preferred_element_type=jnp.float32)


def flip(block):
    return block.astype(jnp.float32).T.astype(block.dtype)


def load_kernel(groups, table_ref, grad_ref, stat_ref, old_ref, out_ref, stat_out, old_out, table_out, held, sems, move_sems):
    copies = [
        pltpu.make_async_copy(source, target, sems.at[i])
        for i, (source, target) in enumerate(
            ((table_ref, table_out), (grad_ref, held), (stat_ref, stat_out), (old_ref, old_out))
        )
    ]
    for copy in copies:
        copy.start()
    group = lax.rem(lax.axis_index("dp"), groups)
    copies[0].wait()
    copies[1].wait()
    moves = []
    for r in range(held.shape[0]):
        moves.append(pltpu.make_async_copy(held.at[r], out_ref.at[table_out[group, 0, r]], move_sems.at[r]))
        moves[-1].start()
    for copy in copies[2:] + moves:
        copy.wait()


def load(groups, table, grad, stat, old):
    size = 2 * grad.size * 2 + 4 * stat.size + 2 * old.size
    return pl.pallas_call(
        functools.partial(load_kernel, groups),
        out_shape=(
            pltpu.HBM(grad.shape, grad.dtype),
            pltpu.VMEM(stat.shape, stat.dtype),
            pltpu.VMEM(old.shape, old.dtype),
            pltpu.SMEM(table.shape, table.dtype),
        ),
        in_specs=[HBM] * 4,
        out_specs=(HBM, VMEM, VMEM, SMEM),
        scratch_shapes=[
            pltpu.VMEM(grad.shape, grad.dtype),
            pltpu.SemaphoreType.DMA((4,)),
            pltpu.SemaphoreType.DMA((grad.shape[0],)),
        ],
        compiler_params=pltpu.CompilerParams(vmem_limit_bytes=4 * MIB),
        cost_estimate=pl.CostEstimate(flops=0, bytes_accessed=size, transcendentals=0),
    )(*(pltpu.with_memory_space_constraint(x, pltpu.HBM) for x in (table, grad, stat, old)))


def from_slots_kernel(groups, table_ref, got_ref, out_ref, sems):
    group = lax.rem(lax.axis_index("dp"), groups)
    copies = []
    for r in range(out_ref.shape[0]):
        slot = table_ref[group, 0, r]
        copies.append(pltpu.make_async_copy(got_ref.at[slot], out_ref.at[r], sems.at[r]))
        copies[-1].start()
    for copy in copies:
        copy.wait()


def from_slots(groups, table, blocks):
    return pl.pallas_call(
        functools.partial(from_slots_kernel, groups),
        out_shape=jax.ShapeDtypeStruct(blocks.shape, blocks.dtype),
        in_specs=[SMEM, VMEM],
        out_specs=HBM,
        scratch_shapes=[pltpu.SemaphoreType.DMA((blocks.shape[0],))],
        compiler_params=pltpu.CompilerParams(vmem_limit_bytes=MIB),
        cost_estimate=pl.CostEstimate(flops=0, bytes_accessed=2 * blocks.size * 2, transcendentals=0),
    )(table, blocks)


def root_kernel(flag_ref, stat_ref, old_ref, root_ref, pack_ref):
    order = stat_ref.shape[0]
    half = order // 2

    @pl.when(flag_ref[0, 0, 0] == 1)
    def _():
        matrix = stat_ref[...]
        rows = lax.broadcasted_iota(jnp.int32, (order, order), 0)
        cols = lax.broadcasted_iota(jnp.int32, (order, order), 1)
        on_diag = rows == cols
        bound = jnp.max(jnp.sum(jnp.abs(matrix), axis=0, keepdims=True), axis=1, keepdims=True)
        scaling = 2.5 / bound
        iterate = scaling * matrix
        root = None
        for turn in range(ITERS):
            step = (jnp.where(on_diag, 5.0 - iterate, -iterate) * 0.25).astype(jnp.bfloat16)
            if turn == 0:
                root = jnp.sqrt(jnp.sqrt(scaling)) * step.astype(jnp.float32)
            else:
                root = dot(root.astype(jnp.bfloat16), step)
            if turn + 1 < ITERS:
                square = dot(step, step).astype(jnp.bfloat16)
                fourth = dot(square, square).astype(jnp.bfloat16)
                iterate = dot(fourth, iterate.astype(jnp.bfloat16))
        root_ref[...] = root.astype(jnp.bfloat16)

    @pl.when(flag_ref[0, 0, 0] != 1)
    def _():
        root_ref[...] = old_ref[...]

    rows = lax.broadcasted_iota(jnp.int32, (half, half), 0)
    cols = lax.broadcasted_iota(jnp.int32, (half, half), 1)
    first = root_ref[0:half, 0:half].astype(jnp.float32)
    second = root_ref[half:order, half:order].astype(jnp.float32)
    pack_ref[0:half, :] = jnp.where(rows <= cols, first, second).astype(jnp.bfloat16)
    pack_ref[half:order, :] = root_ref[half:order, 0:half]
    diagonal = jnp.sum(jnp.where(rows == cols, second, 0.0), axis=0, keepdims=True)
    pack_ref[order : order + 16, :] = jnp.broadcast_to(diagonal, (16, half)).astype(jnp.bfloat16)


def fresh_and_packed(flag, stat, old):
    order = stat.shape[0]
    return pl.pallas_call(
        root_kernel,
        out_shape=(
            jax.ShapeDtypeStruct((order, order), jnp.bfloat16),
            jax.ShapeDtypeStruct((order + 16, order // 2), jnp.bfloat16),
        ),
        in_specs=[SMEM, VMEM, VMEM],
        out_specs=(VMEM, VMEM),
        compiler_params=pltpu.CompilerParams(vmem_limit_bytes=24 * MIB),
        cost_estimate=pl.CostEstimate(flops=8 * order**3, bytes_accessed=9 * order**2, transcendentals=0),
    )(flag, stat, old)


def own_kernel(half_group, root_ref, pack_ref, own_ref, left_ref, right_ref, total_ref):
    order = root_ref.shape[0]
    half = order // 2
    side = lax.axis_index("dp") // half_group
    rows = lax.broadcasted_iota(jnp.int32, (half, half), 0)
    cols = lax.broadcasted_iota(jnp.int32, (half, half), 1)
    tri = pack_ref[0:half, :].astype(jnp.float32)
    tri_flipped = tri.T
    first = jnp.where(rows <= cols, tri, tri_flipped).astype(jnp.bfloat16)

    def own_total(right_own):
        partial = dot(left_ref[...], own_ref[...]).astype(jnp.bfloat16)
        total_ref[...] = dot(partial, right_own)

    @pl.when(side == 0)
    def _():
        left_ref[...] = root_ref[...]
        right_ref[...] = pack_ref[half:order, :]
        own_total(first)

    @pl.when(side != 0)
    def _():
        right_ref[...] = root_ref[0:half, half:order]
        diagonal = pack_ref[order : order + 16, :].astype(jnp.float32)[0:1, :]
        second = jnp.where(rows > cols, tri, jnp.where(rows == cols, diagonal, tri_flipped))
        left_ref[0:half, 0:half] = first
        left_ref[half:order, half:order] = second.astype(jnp.bfloat16)
        left_ref[half:order, 0:half] = pack_ref[half:order, :]
        left_ref[0:half, half:order] = flip(pack_ref[half:order, :])
        own_total(root_ref[half:order, half:order])


def own_part(half_group, root, pack, own):
    order = root.shape[0]
    half = order // 2
    return pl.pallas_call(
        functools.partial(own_kernel, half_group),
        out_shape=(
            jax.ShapeDtypeStruct((order, order), jnp.bfloat16),
            jax.ShapeDtypeStruct((half, half), jnp.bfloat16),
            jax.ShapeDtypeStruct((order, half), jnp.float32),
        ),
        in_specs=[VMEM] * 3,
        out_specs=(VMEM,) * 3,
        compiler_params=pltpu.CompilerParams(vmem_limit_bytes=16 * MIB),
        cost_estimate=pl.CostEstimate(flops=2 * order**3, bytes_accessed=7 * order**2, transcendentals=0),
    )(root, pack, own)


def result_kernel(left_ref, right_ref, total_ref, other_ref, out_ref):
    partial = dot(left_ref[...], other_ref[...]).astype(jnp.bfloat16)
    out_ref[...] = (total_ref[...] + dot(partial, right_ref[...])).astype(jnp.bfloat16)


def result_half(left, right, total, other):
    order = left.shape[0]
    return pl.pallas_call(
        result_kernel,
        out_shape=jax.ShapeDtypeStruct(other.shape, jnp.bfloat16),
        in_specs=[VMEM] * 4,
        out_specs=VMEM,
        compiler_params=pltpu.CompilerParams(vmem_limit_bytes=16 * MIB),
        cost_estimate=pl.CostEstimate(flops=2 * order**3, bytes_accessed=6 * order**2, transcendentals=0),
    )(left, right, total, other)


def stats_kernel(half_group, stat_ref, own_ref, other_ref, out_ref):
    order = stat_ref.shape[0]
    half = order // 2
    side = lax.axis_index("dp") // half_group
    factor = (1.0 - STAT_DECAY) / order

    @pl.when(side == 0)
    def _():
        own, other = own_ref[...], other_ref[...]
        gram = dot(own, own, ((1,), (1,))) + dot(other, other, ((1,), (1,)))
        out_ref[...] = STAT_DECAY * stat_ref[...] + factor * gram

    @pl.when(side != 0)
    def _():
        halves = (other_ref[...], own_ref[...])
        for i in range(2):
            lines = slice(i * half, (i + 1) * half)
            turned = flip(halves[i])
            for j in range(2):
                columns = slice(j * half, (j + 1) * half)
                gram = dot(turned, halves[j])
                out_ref[lines, columns] = STAT_DECAY * stat_ref[lines, columns] + factor * gram


def updated_stats(half_group, stat, own, other):
    order = stat.shape[0]
    return pl.pallas_call(
        functools.partial(stats_kernel, half_group),
        out_shape=jax.ShapeDtypeStruct(stat.shape, jnp.float32),
        in_specs=[VMEM] * 3,
        out_specs=VMEM,
        compiler_params=pltpu.CompilerParams(vmem_limit_bytes=16 * MIB),
        cost_estimate=pl.CostEstimate(flops=2 * order**3, bytes_accessed=10 * order**2, transcendentals=0),
    )(stat, own, other)


def shards(gradient, owner_table, refresh, statistics, inv_roots):
    order = statistics.shape[-1]
    half = order // 2
    dp_count = lax.axis_size("dp")
    half_group = dp_count // 2
    swap = [(source, (source + half_group) % dp_count) for source in range(dp_count)]
    outgoing, stat, old, table = load(
        half_group, owner_table, gradient[0, 0], statistics[0, 0, 0], inv_roots[0, 0, 0]
    )
    received = lax.all_to_all(outgoing, "fsdp", split_axis=0, concat_axis=0, tiled=True)
    own = received.reshape(order, half)
    root, pack = fresh_and_packed(refresh, stat, old)
    other_pack = lax.ppermute(pack, "dp", swap)
    own, pack = lax.optimization_barrier((own, pack))
    other = lax.ppermute(own, "dp", swap)
    left, right, total = own_part(half_group, root, other_pack, own)
    result = result_half(left, right, total, other)
    result, own, other = lax.optimization_barrier((result, own, other))
    returned = lax.all_to_all(result.reshape(outgoing.shape), "fsdp", split_axis=0, concat_axis=0, tiled=True)
    new_stat = updated_stats(half_group, stat, own, other)
    update = from_slots(half_group, table, returned)
    return update[None, None], new_stat[None, None, None]


def solution(mesh):
    return jax.shard_map(
        shards,
        mesh=mesh,
        in_specs=(
            P("dp", "mp", None, "fsdp", None),
            P(None, "mp", None),
            P("dp", "mp", "fsdp"),
            P("dp", "mp", "fsdp", None, None),
            P("dp", "mp", "fsdp", None, None),
        ),
        out_specs=(P("dp", "mp", None, "fsdp", None), P("dp", "mp", "fsdp", None, None)),
        check_vma=False,
    )
```

```python
import functools

import jax
import jax.numpy as jnp
from jax import lax
from jax.experimental import pallas as pl
from jax.experimental.pallas import tpu as pltpu
from jax.sharding import PartitionSpec as P

ITERS = 2
STAT_DECAY = 0.9
MIB = 1024 * 1024
ORDER_16 = (12, 11, 7, 13, 6, 0, 8, 3, 9, 4, 10, 2, 5, 14, 15, 1)

VMEM = pl.BlockSpec(memory_space=pltpu.VMEM)
SMEM = pl.BlockSpec(memory_space=pltpu.SMEM)
HBM = pl.BlockSpec(memory_space=pltpu.HBM)


def dot(left, right, contract=((1,), (0,))):
    return lax.dot_general(left, right, (contract, ((), ())), preferred_element_type=jnp.float32)


def device_order(count):
    return ORDER_16 if count == len(ORDER_16) else tuple(range(count))


def flip(block):
    return block.astype(jnp.float32).T.astype(block.dtype)


def load_kernel(groups, table_ref, grad_ref, stat_ref, old_ref, out_ref, stat_out, old_out, table_out, held, place, sems, move_sems):
    copies = [
        pltpu.make_async_copy(source, target, sems.at[i])
        for i, (source, target) in enumerate(
            ((table_ref, table_out), (grad_ref, held), (stat_ref, stat_out), (old_ref, old_out))
        )
    ]
    for copy in copies:
        copy.start()
    for position, device in enumerate(device_order(held.shape[0])):
        place[device] = position
    group = lax.rem(lax.axis_index("dp"), groups)
    copies[0].wait()
    copies[1].wait()
    moves = []
    for r in range(held.shape[0]):
        moves.append(pltpu.make_async_copy(held.at[r], out_ref.at[place[table_out[group, 0, r]]], move_sems.at[r]))
        moves[-1].start()
    for copy in copies[2:] + moves:
        copy.wait()


def load(groups, table, grad, stat, old):
    size = 2 * grad.size * 2 + 4 * stat.size + 2 * old.size
    return pl.pallas_call(
        functools.partial(load_kernel, groups),
        out_shape=(
            pltpu.HBM(grad.shape, grad.dtype),
            pltpu.VMEM(stat.shape, stat.dtype),
            pltpu.VMEM(old.shape, old.dtype),
            pltpu.SMEM(table.shape, table.dtype),
        ),
        in_specs=[HBM] * 4,
        out_specs=(HBM, VMEM, VMEM, SMEM),
        scratch_shapes=[
            pltpu.VMEM(grad.shape, grad.dtype),
            pltpu.SMEM((grad.shape[0],), jnp.int32),
            pltpu.SemaphoreType.DMA((4,)),
            pltpu.SemaphoreType.DMA((grad.shape[0],)),
        ],
        compiler_params=pltpu.CompilerParams(vmem_limit_bytes=4 * MIB),
        cost_estimate=pl.CostEstimate(flops=0, bytes_accessed=size, transcendentals=0),
    )(*(pltpu.with_memory_space_constraint(x, pltpu.HBM) for x in (table, grad, stat, old)))


def from_slots_kernel(groups, table_ref, got_ref, out_ref, sems):
    group = lax.rem(lax.axis_index("dp"), groups)
    copies = []
    for r in range(out_ref.shape[0]):
        slot = table_ref[group, 0, r]
        copies.append(pltpu.make_async_copy(got_ref.at[slot], out_ref.at[r], sems.at[r]))
        copies[-1].start()
    for copy in copies:
        copy.wait()


def from_slots(groups, table, blocks):
    return pl.pallas_call(
        functools.partial(from_slots_kernel, groups),
        out_shape=jax.ShapeDtypeStruct(blocks.shape, blocks.dtype),
        in_specs=[SMEM, VMEM],
        out_specs=HBM,
        scratch_shapes=[pltpu.SemaphoreType.DMA((blocks.shape[0],))],
        compiler_params=pltpu.CompilerParams(vmem_limit_bytes=MIB),
        cost_estimate=pl.CostEstimate(flops=0, bytes_accessed=2 * blocks.size * 2, transcendentals=0),
    )(table, blocks)


def root_kernel(flag_ref, stat_ref, old_ref, root_ref, pack_ref):
    order = stat_ref.shape[0]
    half = order // 2

    @pl.when(flag_ref[0, 0, 0] == 1)
    def _():
        matrix = stat_ref[...]
        rows = lax.broadcasted_iota(jnp.int32, (order, order), 0)
        cols = lax.broadcasted_iota(jnp.int32, (order, order), 1)
        on_diag = rows == cols
        bound = jnp.max(jnp.sum(jnp.abs(matrix), axis=0, keepdims=True), axis=1, keepdims=True)
        scaling = 2.5 / bound
        iterate = scaling * matrix
        root = None
        for turn in range(ITERS):
            step = (jnp.where(on_diag, 5.0 - iterate, -iterate) * 0.25).astype(jnp.bfloat16)
            if turn == 0:
                root = jnp.sqrt(jnp.sqrt(scaling)) * step.astype(jnp.float32)
            else:
                root = dot(root.astype(jnp.bfloat16), step)
            if turn + 1 < ITERS:
                square = dot(step, step).astype(jnp.bfloat16)
                fourth = dot(square, square).astype(jnp.bfloat16)
                iterate = dot(fourth, iterate.astype(jnp.bfloat16))
        root_ref[...] = root.astype(jnp.bfloat16)

    @pl.when(flag_ref[0, 0, 0] != 1)
    def _():
        root_ref[...] = old_ref[...]

    rows = lax.broadcasted_iota(jnp.int32, (half, half), 0)
    cols = lax.broadcasted_iota(jnp.int32, (half, half), 1)
    first = root_ref[0:half, 0:half].astype(jnp.float32)
    second = root_ref[half:order, half:order].astype(jnp.float32)
    pack_ref[0:half, :] = jnp.where(rows <= cols, first, second).astype(jnp.bfloat16)
    pack_ref[half:order, :] = root_ref[half:order, 0:half]
    diagonal = jnp.sum(jnp.where(rows == cols, second, 0.0), axis=0, keepdims=True)
    pack_ref[order : order + 16, :] = jnp.broadcast_to(diagonal, (16, half)).astype(jnp.bfloat16)


def fresh_and_packed(flag, stat, old):
    order = stat.shape[0]
    return pl.pallas_call(
        root_kernel,
        out_shape=(
            jax.ShapeDtypeStruct((order, order), jnp.bfloat16),
            jax.ShapeDtypeStruct((order + 16, order // 2), jnp.bfloat16),
        ),
        in_specs=[SMEM, VMEM, VMEM],
        out_specs=(VMEM, VMEM),
        compiler_params=pltpu.CompilerParams(vmem_limit_bytes=24 * MIB),
        cost_estimate=pl.CostEstimate(flops=8 * order**3, bytes_accessed=9 * order**2, transcendentals=0),
    )(flag, stat, old)


def own_kernel(half_group, slots, root_ref, pack_ref, own_ref, left_ref, right_ref, total_ref, whole):
    order = root_ref.shape[0]
    half = order // 2
    side = lax.axis_index("dp") // half_group
    rows = lax.broadcasted_iota(jnp.int32, (half, half), 0)
    cols = lax.broadcasted_iota(jnp.int32, (half, half), 1)
    tri = pack_ref[0:half, :].astype(jnp.float32)
    tri_flipped = tri.T
    first = jnp.where(rows <= cols, tri, tri_flipped).astype(jnp.bfloat16)

    slab = order // slots
    arrived = lax.broadcasted_iota(jnp.int32, (1, order), 1)
    source = jnp.zeros_like(arrived)
    for position, device in enumerate(device_order(slots)):
        inside = (arrived >= position * slab) & (arrived < (position + 1) * slab)
        source = jnp.where(inside, arrived + (device - position) * slab, source)
    lines = lax.broadcasted_iota(jnp.int32, (order, order), 0)
    to_arrived = jnp.where(lines == source, 1.0, 0.0).astype(jnp.bfloat16)

    def own_total(right_own):
        partial = dot(left_ref[...], own_ref[...]).astype(jnp.bfloat16)
        total_ref[...] = dot(partial, right_own)

    @pl.when(side == 0)
    def _():
        left_ref[...] = dot(root_ref[...], to_arrived).astype(jnp.bfloat16)
        right_ref[...] = pack_ref[half:order, :]
        own_total(first)

    @pl.when(side != 0)
    def _():
        right_ref[...] = root_ref[0:half, half:order]
        diagonal = pack_ref[order : order + 16, :].astype(jnp.float32)[0:1, :]
        second = jnp.where(rows > cols, tri, jnp.where(rows == cols, diagonal, tri_flipped))
        whole[0:half, 0:half] = first
        whole[half:order, half:order] = second.astype(jnp.bfloat16)
        whole[half:order, 0:half] = pack_ref[half:order, :]
        whole[0:half, half:order] = flip(pack_ref[half:order, :])
        left_ref[...] = dot(whole[...], to_arrived).astype(jnp.bfloat16)
        own_total(root_ref[half:order, half:order])


def own_part(half_group, slots, root, pack, own):
    order = root.shape[0]
    half = order // 2
    return pl.pallas_call(
        functools.partial(own_kernel, half_group, slots),
        out_shape=(
            jax.ShapeDtypeStruct((order, order), jnp.bfloat16),
            jax.ShapeDtypeStruct((half, half), jnp.bfloat16),
            jax.ShapeDtypeStruct((order, half), jnp.float32),
        ),
        in_specs=[VMEM] * 3,
        out_specs=(VMEM,) * 3,
        scratch_shapes=[pltpu.VMEM((order, order), jnp.bfloat16)],
        compiler_params=pltpu.CompilerParams(vmem_limit_bytes=16 * MIB),
        cost_estimate=pl.CostEstimate(flops=4 * order**3, bytes_accessed=7 * order**2, transcendentals=0),
    )(root, pack, own)


def result_kernel(left_ref, right_ref, total_ref, other_ref, out_ref):
    partial = dot(left_ref[...], other_ref[...]).astype(jnp.bfloat16)
    out_ref[...] = (total_ref[...] + dot(partial, right_ref[...])).astype(jnp.bfloat16)


def result_half(left, right, total, other):
    order = left.shape[0]
    return pl.pallas_call(
        result_kernel,
        out_shape=jax.ShapeDtypeStruct(other.shape, jnp.bfloat16),
        in_specs=[VMEM] * 4,
        out_specs=VMEM,
        compiler_params=pltpu.CompilerParams(vmem_limit_bytes=16 * MIB),
        cost_estimate=pl.CostEstimate(flops=2 * order**3, bytes_accessed=6 * order**2, transcendentals=0),
    )(left, right, total, other)


def stats_kernel(half_group, slots, stat_ref, own_ref, other_ref, out_ref, sorted_own, sorted_other):
    order = stat_ref.shape[0]
    half = order // 2
    side = lax.axis_index("dp") // half_group
    factor = (1.0 - STAT_DECAY) / order

    @pl.when(side == 0)
    def _():
        slab = order // slots
        for position, device in enumerate(device_order(slots)):
            arrived = slice(position * slab, (position + 1) * slab)
            lines = slice(device * slab, (device + 1) * slab)
            sorted_own[lines, :] = own_ref[arrived, :]
            sorted_other[lines, :] = other_ref[arrived, :]
        own, other = sorted_own[...], sorted_other[...]
        gram = dot(own, own, ((1,), (1,))) + dot(other, other, ((1,), (1,)))
        out_ref[...] = STAT_DECAY * stat_ref[...] + factor * gram

    @pl.when(side != 0)
    def _():
        halves = (other_ref[...], own_ref[...])
        for i in range(2):
            lines = slice(i * half, (i + 1) * half)
            turned = flip(halves[i])
            for j in range(2):
                columns = slice(j * half, (j + 1) * half)
                gram = dot(turned, halves[j])
                out_ref[lines, columns] = STAT_DECAY * stat_ref[lines, columns] + factor * gram


def updated_stats(half_group, slots, stat, own, other):
    order = stat.shape[0]
    return pl.pallas_call(
        functools.partial(stats_kernel, half_group, slots),
        out_shape=jax.ShapeDtypeStruct(stat.shape, jnp.float32),
        in_specs=[VMEM] * 3,
        out_specs=VMEM,
        scratch_shapes=[pltpu.VMEM(own.shape, own.dtype)] * 2,
        compiler_params=pltpu.CompilerParams(vmem_limit_bytes=16 * MIB),
        cost_estimate=pl.CostEstimate(flops=2 * order**3, bytes_accessed=10 * order**2, transcendentals=0),
    )(stat, own, other)


def shards(gradient, owner_table, refresh, statistics, inv_roots):
    order = statistics.shape[-1]
    half = order // 2
    dp_count = lax.axis_size("dp")
    slots = lax.axis_size("fsdp")
    half_group = dp_count // 2
    swap = [(source, (source + half_group) % dp_count) for source in range(dp_count)]
    outgoing, stat, old, table = load(
        half_group, owner_table, gradient[0, 0], statistics[0, 0, 0], inv_roots[0, 0, 0]
    )
    received = lax.all_to_all(
        outgoing, "fsdp", split_axis=0, concat_axis=0, tiled=True, axis_index_groups=[list(device_order(slots))]
    )
    own = received.reshape(order, half)
    root, pack = fresh_and_packed(refresh, stat, old)
    other_pack = lax.ppermute(pack, "dp", swap)
    own, pack = lax.optimization_barrier((own, pack))
    other = lax.ppermute(own, "dp", swap)
    left, right, total = own_part(half_group, slots, root, other_pack, own)
    result = result_half(left, right, total, other)
    result, own, other = lax.optimization_barrier((result, own, other))
    returned = lax.all_to_all(result.reshape(outgoing.shape), "fsdp", split_axis=0, concat_axis=0, tiled=True)
    new_stat = updated_stats(half_group, slots, stat, own, other)
    update = from_slots(half_group, table, returned)
    return update[None, None], new_stat[None, None, None]


def solution(mesh):
    return jax.shard_map(
        shards,
        mesh=mesh,
        in_specs=(
            P("dp", "mp", None, "fsdp", None),
            P(None, "mp", None),
            P("dp", "mp", "fsdp"),
            P("dp", "mp", "fsdp", None, None),
            P("dp", "mp", "fsdp", None, None),
        ),
        out_specs=(P("dp", "mp", None, "fsdp", None), P("dp", "mp", "fsdp", None, None)),
        check_vma=False,
    )
```

```python
import functools

import jax
import jax.numpy as jnp
from jax import lax
from jax.experimental import pallas as pl
from jax.experimental.pallas import tpu as pltpu
from jax.sharding import PartitionSpec as P

ITERS = 2
STAT_DECAY = 0.9
MIB = 1024 * 1024
ORDER_16 = (12, 11, 7, 13, 6, 0, 8, 3, 9, 4, 10, 2, 5, 14, 15, 1)

VMEM = pl.BlockSpec(memory_space=pltpu.VMEM)
SMEM = pl.BlockSpec(memory_space=pltpu.SMEM)
HBM = pl.BlockSpec(memory_space=pltpu.HBM)


def dot(left, right, contract=((1,), (0,))):
    return lax.dot_general(left, right, (contract, ((), ())), preferred_element_type=jnp.float32)


def device_order(count):
    return ORDER_16 if count == len(ORDER_16) else tuple(range(count))


def flip(block):
    return block.astype(jnp.float32).T.astype(block.dtype)


def load_kernel(groups, table_ref, grad_ref, out_ref, table_out, held, place, sems, move_sems):
    copies = [
        pltpu.make_async_copy(source, target, sems.at[i])
        for i, (source, target) in enumerate(
            ((table_ref, table_out), (grad_ref, held))
        )
    ]
    for copy in copies:
        copy.start()
    for position, device in enumerate(device_order(held.shape[0])):
        place[device] = position
    group = lax.rem(lax.axis_index("dp"), groups)
    copies[0].wait()
    copies[1].wait()
    moves = []
    for r in range(held.shape[0]):
        moves.append(pltpu.make_async_copy(held.at[r], out_ref.at[place[table_out[group, 0, r]]], move_sems.at[r]))
        moves[-1].start()
    for copy in moves:
        copy.wait()


def load(groups, table, grad):
    size = 2 * grad.size * 2
    return pl.pallas_call(
        functools.partial(load_kernel, groups),
        out_shape=(
            pltpu.HBM(grad.shape, grad.dtype),
            pltpu.SMEM(table.shape, table.dtype),
        ),
        in_specs=[HBM] * 2,
        out_specs=(HBM, SMEM),
        scratch_shapes=[
            pltpu.VMEM(grad.shape, grad.dtype),
            pltpu.SMEM((grad.shape[0],), jnp.int32),
            pltpu.SemaphoreType.DMA((2,)),
            pltpu.SemaphoreType.DMA((grad.shape[0],)),
        ],
        compiler_params=pltpu.CompilerParams(vmem_limit_bytes=4 * MIB),
        cost_estimate=pl.CostEstimate(flops=0, bytes_accessed=size, transcendentals=0),
    )(*(pltpu.with_memory_space_constraint(x, pltpu.HBM) for x in (table, grad)))


def from_slots_kernel(groups, table_ref, got_ref, out_ref, sems):
    group = lax.rem(lax.axis_index("dp"), groups)
    copies = []
    for r in range(out_ref.shape[0]):
        slot = table_ref[group, 0, r]
        copies.append(pltpu.make_async_copy(got_ref.at[slot], out_ref.at[r], sems.at[r]))
        copies[-1].start()
    for copy in copies:
        copy.wait()


def from_slots(groups, table, blocks):
    return pl.pallas_call(
        functools.partial(from_slots_kernel, groups),
        out_shape=jax.ShapeDtypeStruct(blocks.shape, blocks.dtype),
        in_specs=[SMEM, VMEM],
        out_specs=HBM,
        scratch_shapes=[pltpu.SemaphoreType.DMA((blocks.shape[0],))],
        compiler_params=pltpu.CompilerParams(vmem_limit_bytes=MIB),
        cost_estimate=pl.CostEstimate(flops=0, bytes_accessed=2 * blocks.size * 2, transcendentals=0),
    )(table, blocks)


def root_kernel(flag_ref, stat_ref, old_ref, root_ref, pack_ref):
    order = stat_ref.shape[0]
    half = order // 2

    @pl.when(flag_ref[0, 0, 0] == 1)
    def _():
        matrix = stat_ref[...]
        rows = lax.broadcasted_iota(jnp.int32, (order, order), 0)
        cols = lax.broadcasted_iota(jnp.int32, (order, order), 1)
        on_diag = rows == cols
        bound = jnp.max(jnp.sum(jnp.abs(matrix), axis=0, keepdims=True), axis=1, keepdims=True)
        scaling = 2.5 / bound
        iterate = scaling * matrix
        root = None
        for turn in range(ITERS):
            step = (jnp.where(on_diag, 5.0 - iterate, -iterate) * 0.25).astype(jnp.bfloat16)
            if turn == 0:
                root = jnp.sqrt(jnp.sqrt(scaling)) * step.astype(jnp.float32)
            else:
                root = dot(root.astype(jnp.bfloat16), step)
            if turn + 1 < ITERS:
                square = dot(step, step).astype(jnp.bfloat16)
                fourth = dot(square, square).astype(jnp.bfloat16)
                iterate = dot(fourth, iterate.astype(jnp.bfloat16))
        root_ref[...] = root.astype(jnp.bfloat16)

    @pl.when(flag_ref[0, 0, 0] != 1)
    def _():
        root_ref[...] = old_ref[...]

    rows = lax.broadcasted_iota(jnp.int32, (half, half), 0)
    cols = lax.broadcasted_iota(jnp.int32, (half, half), 1)
    first = root_ref[0:half, 0:half].astype(jnp.float32)
    second = root_ref[half:order, half:order].astype(jnp.float32)
    pack_ref[0:half, :] = jnp.where(rows <= cols, first, second).astype(jnp.bfloat16)
    pack_ref[half:order, :] = root_ref[half:order, 0:half]
    diagonal = jnp.sum(jnp.where(rows == cols, second, 0.0), axis=0, keepdims=True)
    pack_ref[order : order + 16, :] = jnp.broadcast_to(diagonal, (16, half)).astype(jnp.bfloat16)


def fresh_and_packed(flag, stat, old):
    order = stat.shape[0]
    return pl.pallas_call(
        root_kernel,
        out_shape=(
            jax.ShapeDtypeStruct((order, order), jnp.bfloat16),
            jax.ShapeDtypeStruct((order + 16, order // 2), jnp.bfloat16),
        ),
        in_specs=[SMEM, VMEM, VMEM],
        out_specs=(VMEM, VMEM),
        compiler_params=pltpu.CompilerParams(vmem_limit_bytes=24 * MIB),
        cost_estimate=pl.CostEstimate(flops=8 * order**3, bytes_accessed=9 * order**2, transcendentals=0),
    )(flag, stat, old)


def own_kernel(half_group, slots, root_ref, pack_ref, own_ref, left_ref, right_ref, total_ref, whole):
    order = root_ref.shape[0]
    half = order // 2
    side = lax.axis_index("dp") // half_group
    rows = lax.broadcasted_iota(jnp.int32, (half, half), 0)
    cols = lax.broadcasted_iota(jnp.int32, (half, half), 1)
    tri = pack_ref[0:half, :].astype(jnp.float32)
    tri_flipped = tri.T
    first = jnp.where(rows <= cols, tri, tri_flipped).astype(jnp.bfloat16)

    slab = order // slots
    arrived = lax.broadcasted_iota(jnp.int32, (1, order), 1)
    source = jnp.zeros_like(arrived)
    for position, device in enumerate(device_order(slots)):
        inside = (arrived >= position * slab) & (arrived < (position + 1) * slab)
        source = jnp.where(inside, arrived + (device - position) * slab, source)
    lines = lax.broadcasted_iota(jnp.int32, (order, order), 0)
    to_arrived = jnp.where(lines == source, 1.0, 0.0).astype(jnp.bfloat16)

    def own_total(right_own):
        partial = dot(left_ref[...], own_ref[...]).astype(jnp.bfloat16)
        total_ref[...] = dot(partial, right_own)

    @pl.when(side == 0)
    def _():
        left_ref[...] = dot(root_ref[...], to_arrived).astype(jnp.bfloat16)
        right_ref[...] = pack_ref[half:order, :]
        own_total(first)

    @pl.when(side != 0)
    def _():
        right_ref[...] = root_ref[0:half, half:order]
        diagonal = pack_ref[order : order + 16, :].astype(jnp.float32)[0:1, :]
        second = jnp.where(rows > cols, tri, jnp.where(rows == cols, diagonal, tri_flipped))
        whole[0:half, 0:half] = first
        whole[half:order, half:order] = second.astype(jnp.bfloat16)
        whole[half:order, 0:half] = pack_ref[half:order, :]
        whole[0:half, half:order] = flip(pack_ref[half:order, :])
        left_ref[...] = dot(whole[...], to_arrived).astype(jnp.bfloat16)
        own_total(root_ref[half:order, half:order])


def own_part(half_group, slots, root, pack, own):
    order = root.shape[0]
    half = order // 2
    return pl.pallas_call(
        functools.partial(own_kernel, half_group, slots),
        out_shape=(
            jax.ShapeDtypeStruct((order, order), jnp.bfloat16),
            jax.ShapeDtypeStruct((half, half), jnp.bfloat16),
            jax.ShapeDtypeStruct((order, half), jnp.float32),
        ),
        in_specs=[VMEM] * 3,
        out_specs=(VMEM,) * 3,
        scratch_shapes=[pltpu.VMEM((order, order), jnp.bfloat16)],
        compiler_params=pltpu.CompilerParams(vmem_limit_bytes=16 * MIB),
        cost_estimate=pl.CostEstimate(flops=4 * order**3, bytes_accessed=7 * order**2, transcendentals=0),
    )(root, pack, own)


def result_kernel(left_ref, right_ref, total_ref, other_ref, out_ref):
    partial = dot(left_ref[...], other_ref[...]).astype(jnp.bfloat16)
    out_ref[...] = (total_ref[...] + dot(partial, right_ref[...])).astype(jnp.bfloat16)


def result_half(left, right, total, other):
    order = left.shape[0]
    return pl.pallas_call(
        result_kernel,
        out_shape=jax.ShapeDtypeStruct(other.shape, jnp.bfloat16),
        in_specs=[VMEM] * 4,
        out_specs=VMEM,
        compiler_params=pltpu.CompilerParams(vmem_limit_bytes=16 * MIB),
        cost_estimate=pl.CostEstimate(flops=2 * order**3, bytes_accessed=6 * order**2, transcendentals=0),
    )(left, right, total, other)


def stats_kernel(half_group, slots, stat_ref, own_ref, other_ref, out_ref, sorted_own, sorted_other):
    order = stat_ref.shape[0]
    half = order // 2
    side = lax.axis_index("dp") // half_group
    factor = (1.0 - STAT_DECAY) / order

    @pl.when(side == 0)
    def _():
        slab = order // slots
        for position, device in enumerate(device_order(slots)):
            arrived = slice(position * slab, (position + 1) * slab)
            lines = slice(device * slab, (device + 1) * slab)
            sorted_own[lines, :] = own_ref[arrived, :]
            sorted_other[lines, :] = other_ref[arrived, :]
        own, other = sorted_own[...], sorted_other[...]
        gram = dot(own, own, ((1,), (1,))) + dot(other, other, ((1,), (1,)))
        out_ref[...] = STAT_DECAY * stat_ref[...] + factor * gram

    @pl.when(side != 0)
    def _():
        halves = (other_ref[...], own_ref[...])
        for i in range(2):
            lines = slice(i * half, (i + 1) * half)
            turned = flip(halves[i])
            for j in range(2):
                columns = slice(j * half, (j + 1) * half)
                gram = dot(turned, halves[j])
                out_ref[lines, columns] = STAT_DECAY * stat_ref[lines, columns] + factor * gram


def updated_stats(half_group, slots, stat, own, other):
    order = stat.shape[0]
    return pl.pallas_call(
        functools.partial(stats_kernel, half_group, slots),
        out_shape=jax.ShapeDtypeStruct(stat.shape, jnp.float32),
        in_specs=[VMEM] * 3,
        out_specs=VMEM,
        scratch_shapes=[pltpu.VMEM(own.shape, own.dtype)] * 2,
        compiler_params=pltpu.CompilerParams(vmem_limit_bytes=16 * MIB),
        cost_estimate=pl.CostEstimate(flops=2 * order**3, bytes_accessed=10 * order**2, transcendentals=0),
    )(stat, own, other)


def shards(gradient, owner_table, refresh, statistics, inv_roots):
    order = statistics.shape[-1]
    half = order // 2
    dp_count = lax.axis_size("dp")
    slots = lax.axis_size("fsdp")
    half_group = dp_count // 2
    swap = [(source, (source + half_group) % dp_count) for source in range(dp_count)]
    outgoing, table = load(half_group, owner_table, gradient[0, 0])
    stat, old = statistics[0, 0, 0], inv_roots[0, 0, 0]
    received = lax.all_to_all(
        outgoing, "fsdp", split_axis=0, concat_axis=0, tiled=True, axis_index_groups=[list(device_order(slots))]
    )
    own = received.reshape(order, half)
    root, pack = fresh_and_packed(refresh, stat, old)
    other_pack = lax.ppermute(pack, "dp", swap)
    own, pack = lax.optimization_barrier((own, pack))
    other = lax.ppermute(own, "dp", swap)
    left, right, total = own_part(half_group, slots, root, other_pack, own)
    result = result_half(left, right, total, other)
    result, own, other = lax.optimization_barrier((result, own, other))
    returned = lax.all_to_all(result.reshape(outgoing.shape), "fsdp", split_axis=0, concat_axis=0, tiled=True)
    new_stat = updated_stats(half_group, slots, stat, own, other)
    update = from_slots(half_group, table, returned)
    return update[None, None], new_stat[None, None, None]


def solution(mesh):
    return jax.shard_map(
        shards,
        mesh=mesh,
        in_specs=(
            P("dp", "mp", None, "fsdp", None),
            P(None, "mp", None),
            P("dp", "mp", "fsdp"),
            P("dp", "mp", "fsdp", None, None),
            P("dp", "mp", "fsdp", None, None),
        ),
        out_specs=(P("dp", "mp", None, "fsdp", None), P("dp", "mp", "fsdp", None, None)),
        check_vma=False,
    )
```
